512 devices in a mesh: dp: 32 (over z, core), tensor: 16 (over x, y).
Axes of the slice: x: 4, y: 4, z: 16, core: 2. Of those that a mesh axis runs over, the one named last changes fastest.
Arguments:
- gradient: bfloat16 [32, 3072, 4096], P('dp', None, 'tensor'), may hold values from -66 to 66, as said below
- error_in: bfloat16 [32, 3072, 4096], P('dp', None, 'tensor'), may hold values from -3 to 3
- q_start: float32 [16, 4096], P(None, 'tensor'), may hold values from -6 to 6
Outputs:
- error_out: bfloat16 [32, 3072, 4096], P('dp', None, 'tensor')
- q_factor: float32 [16, 4096], P(None, 'tensor')
The draws below stay inside these ranges and needn't reach their ends.
Inputs may be any that keep to these rules, and one draw needn't show every extreme that they name: Each replica's gradient has independent entries with row and column scales.
All inputs are finite; a program needn't handle non-finite values.
Results may differ from the reference program's by a relative error of at most 0.001.
Values sent between devices are 32-bit elements; how exact they have to be, the bound alone decides.
A program may use at most 64 MiB of HBM per device.

```python
import math
import jax
import jax.numpy as jnp
from jax import lax

COLS = 4096
ROWS = 3072
RANK = 16
ITERS = 2
REPLICAS = 32
N_DP = 32


def draw_gradient(key, part):
    key = jax.random.fold_in(key, 11)
    keys = jax.random.split(key, 4)
    common = jnp.clip(jax.random.normal(keys[0], (1, ROWS, COLS), jnp.float32), -4.0, 4.0)
    own = jnp.clip(jax.random.normal(keys[1], (REPLICAS, ROWS, COLS), jnp.float32), -4.0, 4.0)
    row_scale = jnp.exp(jax.random.uniform(keys[2], (1, ROWS, 1), jnp.float32, math.log(0.5), math.log(3.2)))
    col_scale = jnp.exp(jax.random.uniform(keys[3], (1, 1, COLS), jnp.float32, math.log(0.5), math.log(3.2)))
    return ((common + 0.6 * own) * row_scale * col_scale).astype(jnp.bfloat16)


def level_of(own_key, extent, cuts, low, top_value):
    factor_of, own = 1.0, jax.random.fold_in(own_key, 6)
    for position, blocks in cuts:
        draws = jnp.exp(jax.random.uniform(jax.random.fold_in(own, position), (blocks,), jnp.float32, low / len(cuts), top_value / len(cuts)))
        factor_of = factor_of * jnp.repeat(draws, extent[position] // blocks).reshape([-1 if axis == position else 1 for axis in range(len(extent))])
    return factor_of


def scatter_about(rng, dims, spread, bound, shards=(), dtype=jnp.bfloat16):
    values = jax.random.normal(rng, dims, jnp.float32) * spread
    if len(shards) > 0:
        values = level_of(rng, dims, shards, -0.22, 0.18) * values
    return jnp.clip(values, min=-bound, max=bound).astype(dtype)


def setup_inputs(seed: int = 0) -> dict:
    key_of = jax.random.split(jax.random.key(seed), 4)
    return {
        "gradient": draw_gradient(jax.random.fold_in(key_of[3], 71), 0),
        "error_in": scatter_about(key_of[1], (REPLICAS, ROWS, COLS), 0.5, 3.0, ((0, 32), (2, 16))),
        "q_start": scatter_about(key_of[2], (RANK, COLS), 1.0, 6.0, ((1, 16),), jnp.float32),
    }


def combine(grad_one, error_one):
    return grad_one.astype(jnp.float32) + error_one.astype(jnp.float32)

def reference(gradient, error_in, q_start):
    right = q_start
    left_orth = jnp.zeros((RANK, ROWS), jnp.float32)
    for sweep in range(ITERS):

        def left_step(total, pair):
            accumulated = combine(pair[0], pair[1])
            term = lax.dot_general(right, accumulated, (((1,), (1,)), ((), ())), precision=lax.Precision.HIGHEST)
            return (total + term, None)
        left_sum, unused = lax.scan(left_step, jnp.zeros((RANK, ROWS), jnp.float32), (gradient, error_in))
        left = left_sum / N_DP
        gram = jnp.dot(left, left.T, precision=lax.Precision.HIGHEST)
        lower = jnp.linalg.cholesky(gram)
        left_orth = lax.linalg.triangular_solve(lower, left, left_side=True, lower=True)

        def right_step(total, pair):
            accumulated = combine(pair[0], pair[1])
            return (total + jnp.dot(left_orth, accumulated, precision=lax.Precision.HIGHEST), None)
        right_total, unused = lax.scan(right_step, jnp.zeros((RANK, COLS), jnp.float32), (gradient, error_in))
        right = right_total / N_DP
    approx = jnp.dot(left_orth.T, right, precision=lax.Precision.HIGHEST)
    error_out = lax.map(lambda pair: (combine(pair[0], pair[1]) - approx).astype(jnp.bfloat16), (gradient, error_in))
    return (error_out, right)
```

```python
import jax
import jax.numpy as jnp
from jax import lax
from jax.experimental import pallas as pl
from jax.experimental.pallas import tpu as pltpu
from jax.sharding import PartitionSpec as P

MESH = pl.DeviceIdType.MESH
F32 = jnp.float32
HIGH = lax.Precision.HIGHEST

RANK = 16
LANES = 128
NZ = 16
NT = 16
CHUNKS = 2


def dot_nn(a, b):
    return lax.dot_general(a, b, (((1,), (0,)), ((), ())), precision=HIGH, preferred_element_type=F32)


def dot_nt(a, b):
    return lax.dot_general(a, b, (((1,), (1,)), ((), ())), precision=HIGH, preferred_element_type=F32)


def inverse_factor(gram):
    rows = lax.broadcasted_iota(jnp.int32, (RANK, LANES), 0)
    lanes = lax.broadcasted_iota(jnp.int32, (RANK, LANES), 1)
    both = gram + (lanes == rows + RANK).astype(F32)
    for j in range(RANK):
        column = both[:, j : j + 1]
        scale = 1.0 / jnp.sqrt(column[j : j + 1, :])
        pivot = both[j : j + 1, :] * scale
        step = both - (column * scale) * pivot
        both = jnp.where(rows == j, pivot, jnp.where(rows > j, step, both))
    return both[:, RANK : 2 * RANK]


def compress(
    g_hbm, e_hbm, q_ref, orth_ref, right_ref,
    g_ref, e_ref, own, cross, cross_in, ring, mean, share, shares, term, pair, near, far, halves, gathered,
    load_sem, cross_send, cross_recv, ring_send, ring_recv, share_send, share_recv,
    pair_send, pair_recv, near_send, near_recv, far_send, far_recv, half_send, half_recv,
    gather_send, gather_recv, pass_send, pass_recv,
):
    dp, tensor = lax.axis_index("dp"), lax.axis_index("tensor")
    z, core = dp // 2, dp % 2
    block = own.shape[1]
    other = 1 - core

    loads = [
        pltpu.make_async_copy(g_hbm.at[0], g_ref, load_sem.at[0]),
        pltpu.make_async_copy(e_hbm.at[0], e_ref, load_sem.at[1]),
    ]
    for load in loads:
        load.start()

    sibling = (z * 2 + other, tensor)

    def along_z(hops):
        return (lax.rem(z + hops + NZ, NZ) * 2 + core, tensor)

    def in_plane(k):
        return (dp, lax.rem(tensor + k, NT))

    barrier = pltpu.get_barrier_semaphore()
    pl.semaphore_signal(barrier, inc=1, device_id=sibling, device_id_type=MESH)
    for k in range(1, NZ):
        pl.semaphore_signal(barrier, inc=1, device_id=along_z(k), device_id_type=MESH)
    for k in range(1, NT):
        pl.semaphore_signal(barrier, inc=1, device_id=in_plane(k), device_id_type=MESH)
    mean[...] = jnp.zeros_like(mean)
    for load in loads:
        load.wait()
    pl.semaphore_wait(barrier, NZ + NT - 1)

    def send(src, dst, send_sem, recv_sem, device):
        copy = pltpu.make_async_remote_copy(
            src_ref=src, dst_ref=dst, send_sem=send_sem, recv_sem=recv_sem, device_id=device, device_id_type=MESH
        )
        copy.start()
        return copy

    sent = []

    def accumulated(index):
        rows = pl.ds(pl.multiple_of(index * block, block), block)
        return g_ref[rows, :].astype(F32) + e_ref[rows, :].astype(F32)

    up = [lax.rem(z + 8 - k, NZ) for k in range(8)]
    down = [lax.rem(z + 9 + k, NZ) for k in range(7)]
    order = []
    for k in range(8):
        order.append(up[k])
        if k < 7:
            order.append(down[k])
    order.append(z)
    crossing = []
    for i, j in enumerate(order):
        cross[i] = accumulated(2 * j + other)
        crossing.append(send(cross.at[i], cross_in.at[i], cross_send.at[i], cross_recv.at[i], sibling))
    sent += crossing

    part = block // CHUNKS

    def ring_step(direction, k, target):
        copies = []
        for c in range(CHUNKS):
            rows = pl.ds(c * part, part)
            copies.append(
                send(
                    own.at[target, rows], ring.at[direction, k, rows],
                    ring_send.at[direction, k, c], ring_recv.at[direction, k, c],
                    along_z(1 if direction == 0 else -1),
                )
            )
        return copies

    ring_up, ring_down = [], []
    for i, j in enumerate(order):
        mine = accumulated(2 * j + core)
        crossing[i].wait_recv()
        own[j] = mine + cross_in[i]
        if i == 0:
            ring_up = ring_step(0, 0, j)
        if i == 1:
            ring_down = ring_step(1, 0, j)

    def take(copies, direction, k, target, onward):
        nexts = []
        for c in range(CHUNKS):
            rows = pl.ds(c * part, part)
            copies[c].wait_recv()
            own[target, rows, :] = own[target, rows, :] + ring[direction, k, rows, :]
            if onward:
                nexts.append(
                    send(
                        own.at[target, rows], ring.at[direction, k + 1, rows],
                        ring_send.at[direction, k + 1, c], ring_recv.at[direction, k + 1, c],
                        along_z(1 if direction == 0 else -1),
                    )
                )
        return nexts

    for k in range(1, 9):
        sent += ring_up
        if k < 8:
            ring_up = take(ring_up, 0, k - 1, up[k], True)
        if k < 8:
            sent += ring_down
            if k < 7:
                ring_down = take(ring_down, 1, k - 1, down[k], True)
            else:
                take(ring_down, 1, k - 1, z, False)
        if k == 8:
            take(ring_up, 0, k - 1, z, False)
    mean[0:block, :] = own[z] * (1.0 / 32.0)

    def sum_in_plane(sweep, value):
        share[sweep] = value
        copies = []
        for k in range(1, NT):
            copies.append(
                send(
                    share.at[sweep], shares.at[sweep, tensor],
                    share_send.at[sweep, k], share_recv.at[sweep, k], in_plane(k),
                )
            )
        shares[sweep, tensor] = value
        return copies

    def plane_total(sweep, copies):
        for copy in copies:
            copy.wait_recv()
        total = shares[sweep, 0]
        for k in range(1, NT):
            total = total + shares[sweep, k]
        return total

    def sum_along_z(sweep, value):
        half = term.shape[1] // 2
        term[sweep] = value
        group, place = z // 4, z % 4
        swap = send(
            term.at[sweep, pl.ds(other * half, half)], pair.at[sweep], pair_send.at[sweep], pair_recv.at[sweep], sibling
        )
        sent.append(swap)
        swap.wait_recv()
        near[sweep, place] = term[sweep, pl.ds(core * half, half), :] + pair[sweep]
        copies = []
        for k in range(1, 4):
            device = ((group * 4 + (place + k) % 4) * 2 + core, tensor)
            copies.append(
                send(
                    near.at[sweep, place], near.at[sweep, place],
                    near_send.at[sweep, k], near_recv.at[sweep, k], device,
                )
            )
        for copy in copies:
            copy.wait_recv()
        sent.extend(copies)
        far[sweep, group] = near[sweep, 0] + near[sweep, 1] + near[sweep, 2] + near[sweep, 3]
        copies = []
        for k in (2, 1, 3):
            copies.append(
                send(
                    far.at[sweep, group], far.at[sweep, group],
                    far_send.at[sweep, k], far_recv.at[sweep, k], along_z(4 * k),
                )
            )
        return copies

    def z_total(sweep, copies):
        for copy in copies:
            copy.wait_recv()
        sent.extend(copies)
        halves[sweep, core] = far[sweep, 0] + far[sweep, 1] + far[sweep, 2] + far[sweep, 3]
        swap = send(
            halves.at[sweep, core], halves.at[sweep, core], half_send.at[sweep], half_recv.at[sweep], sibling
        )
        swap.wait_recv()
        sent.append(swap)

    def z_term(left):
        wide = dot_nn(left, mean[...])
        gram = jnp.concatenate([dot_nt(left, left), jnp.zeros((RANK, LANES - RANK), F32)], axis=1)
        return jnp.concatenate([wide[:, :LANES], gram[:8], wide[:, LANES:], gram[8:]], axis=0)

    copies = sum_in_plane(0, dot_nt(q_ref[...], mean[...]))
    left = plane_total(0, copies)
    sent += copies
    z_total(0, sum_along_z(0, z_term(left)))
    right = jnp.concatenate([halves[0, 0, 0:RANK, :], halves[0, 1, 0:RANK, :]], axis=1)
    copies = sum_in_plane(1, dot_nt(right, mean[...]))
    gram = jnp.concatenate([halves[0, 0, RANK:, :], halves[0, 1, RANK:, :]], axis=0)
    inverse = inverse_factor(gram)

    left = dot_nn(inverse, plane_total(1, copies))
    sent += copies
    gathered[dp] = left
    passing = [send(gathered.at[dp], gathered.at[dp], pass_send.at[0], pass_recv.at[0], sibling)]
    gathering = {}
    for k in sorted(range(1, NZ), key=lambda k: -min(k, NZ - k)):
        gathering[k] = send(
            gathered.at[dp], gathered.at[dp], gather_send.at[k], gather_recv.at[k], along_z(k)
        )
    far_copies = sum_along_z(1, z_term(left))
    for k in sorted(range(1, NZ), key=lambda k: min(k, NZ - k)):
        gathering[k].wait_recv()
        origin = lax.rem(z - k + NZ, NZ) * 2 + core
        passing.append(
            send(gathered.at[origin], gathered.at[origin], pass_send.at[k], pass_recv.at[k], sibling)
        )
    for copy in passing:
        copy.wait_recv()
    sent += passing + list(gathering.values())
    gram = jnp.zeros((RANK, RANK), F32)
    for d in range(2 * NZ):
        gram = gram + dot_nt(gathered[d], gathered[d])
    gram = jnp.concatenate([gram, jnp.zeros((RANK, LANES - RANK), F32)], axis=1)
    inverse = inverse_factor(gram)
    for d in range(2 * NZ):
        orth_ref[d] = dot_nn(inverse, gathered[d])
    z_total(1, far_copies)
    right = jnp.concatenate([halves[1, 0, 0:RANK, :], halves[1, 1, 0:RANK, :]], axis=1)
    right_ref[...] = dot_nn(inverse, right)
    for copy in sent:
        copy.wait_send()


def residual(g_ref, e_ref, orth_ref, right_ref, out_ref):
    block = g_ref.shape[1] // orth_ref.shape[0]
    right = right_ref[...]
    for b in range(orth_ref.shape[0]):
        rows = slice(b * block, (b + 1) * block)
        approx = lax.dot_general(
            orth_ref[b], right, (((0,), (0,)), ((), ())), precision=HIGH, preferred_element_type=F32
        )
        total = g_ref[0, rows, :].astype(F32) + e_ref[0, rows, :].astype(F32)
        out_ref[0, rows, :] = (total - approx[:block]).astype(jnp.bfloat16)


def per_device(gradient, error_in, q_start):
    rows, columns = gradient.shape[1:]
    block = rows // (2 * NZ)
    hbm = pl.BlockSpec(memory_space=pl.ANY)
    vmem = pl.BlockSpec(memory_space=pltpu.VMEM)
    dma = pltpu.SemaphoreType.DMA
    half = RANK + 8
    orth, right = pl.pallas_call(
        compress,
        out_shape=[
            jax.ShapeDtypeStruct((2 * NZ, RANK, LANES), F32),
            jax.ShapeDtypeStruct((RANK, columns), F32),
        ],
        in_specs=[hbm, hbm, vmem],
        out_specs=[vmem, vmem],
        scratch_shapes=[
            pltpu.VMEM((rows, columns), jnp.bfloat16),
            pltpu.VMEM((rows, columns), jnp.bfloat16),
            pltpu.VMEM((NZ, block, columns), F32),
            pltpu.VMEM((NZ, block, columns), F32),
            pltpu.VMEM((NZ, block, columns), F32),
            pltpu.VMEM((2, 8, block, columns), F32),
            pltpu.VMEM((LANES, columns), F32),
            pltpu.VMEM((2, RANK, LANES), F32),
            pltpu.VMEM((2, NT, RANK, LANES), F32),
            pltpu.VMEM((2, 2 * half, LANES), F32),
            pltpu.VMEM((2, half, LANES), F32),
            pltpu.VMEM((2, 4, half, LANES), F32),
            pltpu.VMEM((2, 4, half, LANES), F32),
            pltpu.VMEM((2, 2, half, LANES), F32),
            pltpu.VMEM((2 * NZ, RANK, LANES), F32),
            dma((2,)),
            dma((NZ,)), dma((NZ,)),
            dma((2, 8, CHUNKS)), dma((2, 8, CHUNKS)),
            dma((2, NT)), dma((2, NT)),
            dma((2,)), dma((2,)),
            dma((2, 4)), dma((2, 4)),
            dma((2, 4)), dma((2, 4)),
            dma((2,)), dma((2,)),
            dma((NZ,)), dma((NZ,)),
            dma((NZ,)), dma((NZ,)),
        ],
        compiler_params=pltpu.CompilerParams(
            collective_id=0, has_side_effects=True, vmem_limit_bytes=24 * 2**20
        ),
        name="compress",
    )(gradient, error_in, q_start)
    steps = 4
    tile = rows // steps
    error_out = pl.pallas_call(
        residual,
        grid=(steps,),
        out_shape=jax.ShapeDtypeStruct(gradient.shape, gradient.dtype),
        in_specs=[
            pl.BlockSpec((1, tile, columns), lambda i: (0, i, 0)),
            pl.BlockSpec((1, tile, columns), lambda i: (0, i, 0)),
            pl.BlockSpec((2 * NZ // steps, RANK, LANES), lambda i: (i, 0, 0)),
            pl.BlockSpec((RANK, columns), lambda i: (0, 0)),
        ],
        out_specs=pl.BlockSpec((1, tile, columns), lambda i: (0, i, 0)),
        name="residual",
    )(gradient, error_in, orth, right)
    return (error_out, right)


def solution(mesh):
    placed = (P("dp", None, "tensor"), P("dp", None, "tensor"), P(None, "tensor"))
    return jax.shard_map(
        per_device,
        mesh=mesh,
        in_specs=placed,
        out_specs=(P("dp", None, "tensor"), P(None, "tensor")),
        check_vma=False,
    )
```

```python
import jax
import jax.numpy as jnp
from jax import lax
from jax.experimental import pallas as pl
from jax.experimental.pallas import tpu as pltpu
from jax.sharding import PartitionSpec as P

MESH = pl.DeviceIdType.MESH
F32 = jnp.float32
HIGH = lax.Precision.HIGHEST

RANK = 16
LANES = 128
NZ = 16
NT = 16
CHUNKS = 4


def dot_nn(a, b):
    return lax.dot_general(a, b, (((1,), (0,)), ((), ())), precision=HIGH, preferred_element_type=F32)


def dot_nt(a, b):
    return lax.dot_general(a, b, (((1,), (1,)), ((), ())), precision=HIGH, preferred_element_type=F32)


def inverse_factor(gram):
    rows = lax.broadcasted_iota(jnp.int32, (RANK, LANES), 0)
    lanes = lax.broadcasted_iota(jnp.int32, (RANK, LANES), 1)
    both = gram + (lanes == rows + RANK).astype(F32)
    for j in range(RANK):
        column = both[:, j : j + 1]
        scale = 1.0 / jnp.sqrt(column[j : j + 1, :])
        pivot = both[j : j + 1, :] * scale
        step = both - (column * scale) * pivot
        both = jnp.where(rows == j, pivot, jnp.where(rows > j, step, both))
    return both[:, RANK : 2 * RANK]


def split_three(value):
    top = value.astype(jnp.bfloat16)
    rest = value - top.astype(F32)
    middle = rest.astype(jnp.bfloat16)
    return top, middle, (rest - middle.astype(F32)).astype(jnp.bfloat16)


def compress(
    g_hbm, e_hbm, q_ref, out_ref, right_ref,
    g_ref, e_ref, own, cross, cross_in, ring, mean, share, shares, term, pair, near, far, halves, relay, gathered,
    load_sem, cross_send, cross_recv, ring_send, ring_recv, share_send, share_recv,
    pair_send, pair_recv, near_send, near_recv, far_send, far_recv, half_send, half_recv,
    relay_send, relay_recv, gather_send, gather_recv, pass_send, pass_recv, known_one, known_two,
):
    dp, tensor = lax.axis_index("dp"), lax.axis_index("tensor")
    z, core = dp // 2, dp % 2
    x, y = tensor // 4, tensor % 4
    block = own.shape[1]
    other = 1 - core

    up = [lax.rem(z + 8 - k, NZ) for k in range(8)]
    down = [lax.rem(z + 9 + k, NZ) for k in range(7)]
    order = []
    for k in range(8):
        order.append(up[k])
        if k < 7:
            order.append(down[k])
    order.append(z)

    loads = []
    for i, j in enumerate(order):
        rows = pl.ds(pl.multiple_of(j * (2 * block), 2 * block), 2 * block)
        loads.append(
            (
                pltpu.make_async_copy(g_hbm.at[0, rows], g_ref.at[rows], load_sem.at[0, i]),
                pltpu.make_async_copy(e_hbm.at[0, rows], e_ref.at[rows], load_sem.at[1, i]),
            )
        )
        for load in loads[i]:
            load.start()

    sibling = (z * 2 + other, tensor)

    def along_z(hops):
        return (lax.rem(z + hops + NZ, NZ) * 2 + core, tensor)

    def in_plane(k):
        return (dp, lax.rem(tensor + k, NT))

    def hop(dx, dy):
        return (dp, lax.rem(x + dx + 4, 4) * 4 + lax.rem(y + dy + 4, 4))

    steps = [hop(1, 0), hop(-1, 0), hop(0, 1), hop(0, -1)]
    neighbours = [sibling, along_z(1), along_z(-1)] + steps
    barrier = pltpu.get_barrier_semaphore()
    for device in neighbours:
        pl.semaphore_signal(barrier, inc=1, device_id=device, device_id_type=MESH)
    mean[...] = jnp.zeros_like(mean)
    pl.semaphore_wait(barrier, len(neighbours))
    for device in steps:
        pl.semaphore_signal(known_one, inc=1, device_id=device, device_id_type=MESH)

    sent = []

    def send(src, dst, send_sem, recv_sem, device):
        copy = pltpu.make_async_remote_copy(
            src_ref=src, dst_ref=dst, send_sem=send_sem, recv_sem=recv_sem, device_id=device, device_id_type=MESH
        )
        copy.start()
        sent.append(copy)
        return copy

    def accumulated(index):
        rows = pl.ds(pl.multiple_of(index * block, block), block)
        return g_ref[rows, :].astype(F32) + e_ref[rows, :].astype(F32)

    part = block // CHUNKS

    def forward(direction, k, target, c):
        rows = pl.ds(c * part, part)
        return send(
            own.at[target, rows], ring.at[direction, k, rows],
            ring_send.at[direction, k, c], ring_recv.at[direction, k, c],
            along_z(1 if direction == 0 else -1),
        )

    crossing = []

    def cross_over(i):
        for load in loads[i]:
            load.wait()
        cross[i] = accumulated(2 * order[i] + other)
        crossing.append(send(cross.at[i], cross_in.at[i], cross_send.at[i], cross_recv.at[i], sibling))

    def add_cores(i):
        mine = accumulated(2 * order[i] + core)
        crossing[i].wait_recv()
        own[order[i]] = mine + cross_in[i]

    cross_over(0)
    cross_over(1)
    cross_over(2)
    cross_over(3)
    add_cores(0)
    ring_up = [forward(0, 0, up[0], c) for c in range(CHUNKS)]
    add_cores(1)
    ring_down = [forward(1, 0, down[0], c) for c in range(CHUNKS)]
    for i in range(4, 16):
        cross_over(i)
    for i in range(2, 16):
        add_cores(i)

    def take(copies, direction, k, target, c, onward):
        rows = pl.ds(c * part, part)
        copies[c].wait_recv()
        own[target, rows, :] = own[target, rows, :] + ring[direction, k, rows, :]
        if onward:
            copies[c] = forward(direction, k + 1, target, c)

    for k in range(1, 9):
        for c in range(CHUNKS):
            take(ring_up, 0, k - 1, up[k] if k < 8 else z, c, k < 8)
            if k < 8:
                take(ring_down, 1, k - 1, down[k] if k < 7 else z, c, k < 7)
        if k == 2:
            pl.semaphore_wait(known_one, len(steps))
            for device in [hop(2, 0), hop(0, 2), hop(1, 1), hop(1, -1), hop(-1, 1), hop(-1, -1)]:
                pl.semaphore_signal(known_two, inc=1, device_id=device, device_id_type=MESH)
    pl.semaphore_wait(known_two, 6)
    mean[0:block, :] = own[z] * (1.0 / 32.0)

    def sum_in_plane(sweep, value):
        share[sweep] = value
        copies = []
        for k in range(1, NT):
            copies.append(
                send(
                    share.at[sweep], shares.at[sweep, tensor],
                    share_send.at[sweep, k], share_recv.at[sweep, k], in_plane(k),
                )
            )
        shares[sweep, tensor] = value
        return copies

    def plane_total(sweep, copies):
        for copy in copies:
            copy.wait_recv()
        total = shares[sweep, 0]
        for k in range(1, NT):
            total = total + shares[sweep, k]
        return total

    group, place = z // 4, z % 4

    def sum_near(sweep, value):
        half = value.shape[0] // 2
        term[sweep, 0 : 2 * half, :] = value
        kept = pl.ds(0, half)
        swap = send(
            term.at[sweep, pl.ds(other * half, half)], pair.at[sweep, kept],
            pair_send.at[sweep], pair_recv.at[sweep], sibling,
        )
        swap.wait_recv()
        near[sweep, place, kept, :] = term[sweep, pl.ds(core * half, half), :] + pair[sweep, kept, :]
        copies = []
        for k in range(1, 4):
            device = ((group * 4 + (place + k) % 4) * 2 + core, tensor)
            copies.append(
                send(
                    near.at[sweep, place, kept], near.at[sweep, place, kept],
                    near_send.at[sweep, k], near_recv.at[sweep, k], device,
                )
            )
        for copy in copies:
            copy.wait_recv()
        far[sweep, group, kept, :] = (
            near[sweep, 0, kept, :] + near[sweep, 1, kept, :] + near[sweep, 2, kept, :] + near[sweep, 3, kept, :]
        )
        copies = []
        for k in (2, 1, 3):
            copies.append(
                send(
                    far.at[sweep, group, kept], far.at[sweep, group, kept],
                    far_send.at[sweep, k], far_recv.at[sweep, k], along_z(4 * k),
                )
            )
        return copies

    def sum_far(sweep, half, copies):
        kept = pl.ds(0, half)
        for copy in copies:
            copy.wait_recv()
        halves[sweep, core, kept, :] = (
            far[sweep, 0, kept, :] + far[sweep, 1, kept, :] + far[sweep, 2, kept, :] + far[sweep, 3, kept, :]
        )
        return send(
            halves.at[sweep, core, kept], halves.at[sweep, core, kept],
            half_send.at[sweep], half_recv.at[sweep], sibling,
        )

    pad = jnp.zeros((RANK, LANES - RANK), F32)

    copies = sum_in_plane(0, dot_nt(q_ref[...], mean[...]))
    left = plane_total(0, copies)
    wide = dot_nn(left, mean[...])
    gram = jnp.concatenate([dot_nt(left, left), pad], axis=1)
    value = jnp.concatenate([wide[:, :LANES], gram[:8], wide[:, LANES:], gram[8:]], axis=0)
    sum_far(0, RANK + 8, sum_near(0, value)).wait_recv()
    right = jnp.concatenate([halves[0, 0, 0:RANK, :], halves[0, 1, 0:RANK, :]], axis=1)
    copies = sum_in_plane(1, dot_nt(right, mean[...]))
    gram = jnp.concatenate([halves[0, 0, RANK : RANK + 8, :], halves[0, 1, RANK : RANK + 8, :]], axis=0)
    inverse = inverse_factor(gram)

    left = dot_nn(inverse, plane_total(1, copies))
    gathered[dp] = left

    def relayed():
        return pltpu.make_async_remote_copy(
            src_ref=gathered.at[dp], dst_ref=relay, send_sem=relay_send, recv_sem=relay_recv,
            device_id=along_z(tensor), device_id_type=MESH,
        )

    @pl.when(tensor > 0)
    def _():
        relayed().start()

    def hand_done():
        @pl.when(tensor > 0)
        def _():
            for k in range(1, NT):
                handed(k).wait_send()

    passing = [send(gathered.at[dp], gathered.at[dp], pass_send.at[0], pass_recv.at[0], sibling)]
    wide = dot_nn(left, mean[...])
    far_copies = sum_near(1, jnp.concatenate([wide[:, :LANES], wide[:, LANES:]], axis=0))

    origin = lax.rem(z - tensor + NZ, NZ) * 2 + core

    def handed(k):
        return pltpu.make_async_remote_copy(
            src_ref=relay, dst_ref=gathered.at[origin], send_sem=gather_send.at[k],
            recv_sem=gather_recv.at[tensor], device_id=in_plane(k), device_id_type=MESH,
        )

    @pl.when(tensor > 0)
    def _():
        relayed().wait()
        for k in range(1, NT):
            handed(k).start()
        gathered[origin] = relay[...]

    for k in range(1, NT):
        source = lax.rem(z - k + NZ, NZ) * 2 + core

        @pl.when(tensor != k)
        def _():
            pltpu.make_async_remote_copy(
                src_ref=relay, dst_ref=gathered.at[source], send_sem=gather_send.at[k],
                recv_sem=gather_recv.at[k], device_id=in_plane(k), device_id_type=MESH,
            ).wait_recv()

        passing.append(
            send(gathered.at[source], gathered.at[source], pass_send.at[k], pass_recv.at[k], sibling)
        )
    for copy in passing:
        copy.wait_recv()
    gram = jnp.zeros((RANK, RANK), F32)
    for d in range(2 * NZ):
        gram = gram + dot_nt(gathered[d], gathered[d])
    inverse = inverse_factor(jnp.concatenate([gram, pad], axis=1))
    last = sum_far(1, RANK, far_copies)
    tops, middles, lows = [], [], []
    for d in range(2 * NZ):
        orth = dot_nn(inverse, gathered[d])
        top, middle, low = split_three(orth)
        tops.append(jnp.concatenate([top, middle, top, low, middle, top], axis=0))
    last.wait_recv()
    right = dot_nn(inverse, jnp.concatenate([halves[1, 0, 0:RANK, :], halves[1, 1, 0:RANK, :]], axis=1))
    right_ref[...] = right
    top, middle, low = split_three(right)
    stacked = jnp.concatenate([top, top, middle, top, middle, low], axis=0)
    for d in range(2 * NZ):
        rows = pl.ds(d * block, block)
        approx = lax.dot_general(tops[d], stacked, (((0,), (0,)), ((), ())), preferred_element_type=F32)
        total = g_ref[rows, :].astype(F32) + e_ref[rows, :].astype(F32)
        out_ref[0, rows, :] = (total - approx[:block]).astype(jnp.bfloat16)

    hand_done()
    for copy in sent:
        copy.wait_send()


def per_device(gradient, error_in, q_start):
    rows, columns = gradient.shape[1:]
    block = rows // (2 * NZ)
    hbm = pl.BlockSpec(memory_space=pltpu.HBM)
    vmem = pl.BlockSpec(memory_space=pltpu.VMEM)
    dma = pltpu.SemaphoreType.DMA
    half = RANK + 8
    return pl.pallas_call(
        compress,
        out_shape=[
            jax.ShapeDtypeStruct(gradient.shape, gradient.dtype),
            jax.ShapeDtypeStruct((RANK, columns), F32),
        ],
        in_specs=[hbm, hbm, vmem],
        out_specs=[vmem, vmem],
        scratch_shapes=[
            pltpu.VMEM((rows, columns), jnp.bfloat16),
            pltpu.VMEM((rows, columns), jnp.bfloat16),
            pltpu.VMEM((NZ, block, columns), F32),
            pltpu.VMEM((NZ, block, columns), F32),
            pltpu.VMEM((NZ, block, columns), F32),
            pltpu.VMEM((2, 8, block, columns), F32),
            pltpu.VMEM((LANES, columns), F32),
            pltpu.VMEM((2, RANK, LANES), F32),
            pltpu.VMEM((2, NT, RANK, LANES), F32),
            pltpu.VMEM((2, 2 * half, LANES), F32),
            pltpu.VMEM((2, half, LANES), F32),
            pltpu.VMEM((2, 4, half, LANES), F32),
            pltpu.VMEM((2, 4, half, LANES), F32),
            pltpu.VMEM((2, 2, half, LANES), F32),
            pltpu.VMEM((RANK, LANES), F32),
            pltpu.VMEM((2 * NZ, RANK, LANES), F32),
            dma((2, NZ)),
            dma((NZ,)), dma((NZ,)),
            dma((2, 8, CHUNKS)), dma((2, 8, CHUNKS)),
            dma((2, NT)), dma((2, NT)),
            dma((2,)), dma((2,)),
            dma((2, 4)), dma((2, 4)),
            dma((2, 4)), dma((2, 4)),
            dma((2,)), dma((2,)),
            dma, dma,
            dma((NT,)), dma((NT,)),
            dma((NZ,)), dma((NZ,)),
            pltpu.SemaphoreType.REGULAR, pltpu.SemaphoreType.REGULAR,
        ],
        compiler_params=pltpu.CompilerParams(
            collective_id=0, has_side_effects=True, vmem_limit_bytes=52 * 2**20
        ),
        name="compress",
    )(gradient, error_in, q_start)


def solution(mesh):
    placed = (P("dp", None, "tensor"), P("dp", None, "tensor"), P(None, "tensor"))
    return jax.shard_map(
        per_device,
        mesh=mesh,
        in_specs=placed,
        out_specs=(P("dp", None, "tensor"), P(None, "tensor")),
        check_vma=False,
    )
```

```python
import jax
import jax.numpy as jnp
from jax import lax
from jax.experimental import pallas as pl
from jax.experimental.pallas import tpu as pltpu
from jax.sharding import PartitionSpec as P

MESH = pl.DeviceIdType.MESH
F32 = jnp.float32
HIGH = lax.Precision.HIGHEST

RANK = 16
LANES = 128
NZ = 16
NT = 16
CHUNKS = 4


def dot_nn(a, b):
    return lax.dot_general(a, b, (((1,), (0,)), ((), ())), precision=HIGH, preferred_element_type=F32)


def dot_nt(a, b):
    return lax.dot_general(a, b, (((1,), (1,)), ((), ())), precision=HIGH, preferred_element_type=F32)


def inverse_factor(gram):
    rows = lax.broadcasted_iota(jnp.int32, (RANK, LANES), 0)
    lanes = lax.broadcasted_iota(jnp.int32, (RANK, LANES), 1)
    both = gram + (lanes == rows + RANK).astype(F32)
    for j in range(RANK):
        column = both[:, j : j + 1]
        scale = 1.0 / jnp.sqrt(column[j : j + 1, :])
        pivot = both[j : j + 1, :] * scale
        step = both - (column * scale) * pivot
        both = jnp.where(rows == j, pivot, jnp.where(rows > j, step, both))
    return both[:, RANK : 2 * RANK]


def split_three(value):
    top = value.astype(jnp.bfloat16)
    rest = value - top.astype(F32)
    middle = rest.astype(jnp.bfloat16)
    return top, middle, (rest - middle.astype(F32)).astype(jnp.bfloat16)


def compress(
    g_hbm, e_hbm, q_hbm, out_ref, right_ref,
    g_ref, e_ref, q_ref, early, early_in, early_sum, plane_in, first, own, cross, cross_in, ring, mean_top, mean_middle, mean_low, share, shares, term, pair, near, far, halves, relay, gathered, turned,
    load_sem, cross_send, cross_recv, ring_send, ring_recv, share_send, share_recv,
    pair_send, pair_recv, near_send, near_recv, far_send, far_recv, half_send, half_recv,
    early_send, early_recv, plane_send, plane_recv, owner_send, owner_recv, q_sem,
    relay_send, relay_recv, gather_send, gather_recv, pass_send, pass_recv, known_one, known_two, known_z,
):
    dp, tensor = lax.axis_index("dp"), lax.axis_index("tensor")
    z, core = dp // 2, dp % 2
    x, y = tensor // 4, tensor % 4
    mean_parts = (mean_top, mean_middle, mean_low)
    block = own.shape[1]
    other = 1 - core

    up = [lax.rem(z + 8 - k, NZ) for k in range(8)]
    down = [lax.rem(z + 9 + k, NZ) for k in range(7)]
    order = []
    for k in range(8):
        order.append(up[k])
        if k < 7:
            order.append(down[k])
    order.append(z)

    q_load = pltpu.make_async_copy(q_hbm, q_ref, q_sem)
    loads = []
    for i, j in enumerate(order):
        rows = pl.ds(pl.multiple_of(j * (2 * block), 2 * block), 2 * block)
        loads.append(
            (
                pltpu.make_async_copy(g_hbm.at[0, rows], g_ref.at[rows], load_sem.at[0, i]),
                pltpu.make_async_copy(e_hbm.at[0, rows], e_ref.at[rows], load_sem.at[1, i]),
            )
        )
        for load in loads[i]:
            load.start()
        if i == 1:
            q_load.start()

    sibling = (z * 2 + other, tensor)

    def along_z(hops):
        return (lax.rem(z + hops + NZ, NZ) * 2 + core, tensor)

    def in_plane(k):
        return (dp, lax.rem(tensor + k, NT))

    def hop(dx, dy):
        return (dp, lax.rem(x + dx + 4, 4) * 4 + lax.rem(y + dy + 4, 4))

    steps = [hop(1, 0), hop(-1, 0), hop(0, 1), hop(0, -1)]
    neighbours = [sibling, along_z(1), along_z(-1)] + steps
    barrier = pltpu.get_barrier_semaphore()
    for device in neighbours:
        pl.semaphore_signal(barrier, inc=1, device_id=device, device_id_type=MESH)
    for part_ref in mean_parts:
        part_ref[...] = jnp.zeros_like(part_ref)
    early[...] = jnp.zeros_like(early)
    early_sum[...] = jnp.zeros_like(early_sum)

    def accumulated(index):
        rows = pl.ds(pl.multiple_of(index * block, block), block)
        return g_ref[rows, :].astype(F32) + e_ref[rows, :].astype(F32)

    def wait_load(i):
        for load in loads[i]:
            load.wait()

    for i in range(4):
        wait_load(i)
        cross[i] = accumulated(2 * order[i] + other)
    pl.semaphore_wait(barrier, len(neighbours))

    def tell(semaphore, devices):
        for device in devices:
            pl.semaphore_signal(semaphore, inc=1, device_id=device, device_id_type=MESH)

    corners = [hop(2, 0), hop(0, 2), hop(1, 1), hop(1, -1), hop(-1, 1), hop(-1, -1)]
    tell(known_one, steps)
    tell(known_z.at[0], [along_z(1), along_z(-1)])

    sent = []

    def send(src, dst, send_sem, recv_sem, device):
        copy = pltpu.make_async_remote_copy(
            src_ref=src, dst_ref=dst, send_sem=send_sem, recv_sem=recv_sem, device_id=device, device_id_type=MESH
        )
        copy.start()
        sent.append(copy)
        return copy

    part = block // CHUNKS

    def forward(direction, k, target, c):
        rows = pl.ds(c * part, part)
        return send(
            own.at[target, rows], ring.at[direction, k, rows],
            ring_send.at[direction, k, c], ring_recv.at[direction, k, c],
            along_z(1 if direction == 0 else -1),
        )

    crossing = []

    def cross_over(i):
        if i >= 4:
            cross[i] = accumulated(2 * order[i] + other)
        crossing.append(send(cross.at[i], cross_in.at[i], cross_send.at[i], cross_recv.at[i], sibling))

    def add_cores(i):
        mine = accumulated(2 * order[i] + core)
        crossing[i].wait_recv()
        own[order[i]] = mine + cross_in[i]

    for i in range(4):
        cross_over(i)
    q_load.wait()
    q_parts = jnp.concatenate(split_three(q_ref[...]), axis=0)

    def early_term(j):
        for half in range(2):
            rows = pl.ds(pl.multiple_of((2 * j + half) * block, block), block)
            dims = (((1,), (1,)), ((), ()))
            three = lax.dot_general(q_parts, g_ref[rows, :], dims, preferred_element_type=F32)
            three = three + lax.dot_general(q_parts, e_ref[rows, :], dims, preferred_element_type=F32)
            early[j, half, :, 0:block] = three[:RANK] + (three[RANK : 2 * RANK] + three[2 * RANK :])

    for i in range(0, 4):
        early_term(order[i])
    add_cores(0)
    ring_up = [forward(0, 0, up[0], c) for c in range(CHUNKS)]
    add_cores(1)
    ring_down = [forward(1, 0, down[0], c) for c in range(CHUNKS)]
    for i in range(4, 8):
        wait_load(i)
        cross_over(i)
    for i in range(8, 16):
        wait_load(i)
    for i in range(4, 16):
        early_term(order[i])
    add_cores(2)
    add_cores(3)
    pl.semaphore_wait(known_one, len(steps))
    pl.semaphore_wait(known_z.at[0], 2)
    tell(known_two, corners)
    tell(known_z.at[1], [along_z(2), along_z(-2)])

    def take(copies, direction, k, target, c, onward):
        rows = pl.ds(c * part, part)
        copies[c].wait_recv()
        own[target, rows, :] = own[target, rows, :] + ring[direction, k, rows, :]
        if onward:
            copies[c] = forward(direction, k + 1, target, c)

    def to_owner(half):
        return pltpu.make_async_remote_copy(
            src_ref=early_sum.at[half], dst_ref=plane_in.at[dp], send_sem=plane_send.at[half],
            recv_sem=plane_recv.at[dp], device_id=(2 * tensor + half, tensor), device_id_type=MESH,
        )

    def from_owner(n):
        return pltpu.make_async_remote_copy(
            src_ref=first, dst_ref=first, send_sem=owner_send.at[n], recv_sem=owner_recv,
            device_id=in_plane(n), device_id_type=MESH,
        )

    def early_done():
        for half in range(2):

            @pl.when(dp != 2 * tensor + half)
            def _():
                to_owner(half).wait_send()

        @pl.when(z == tensor)
        def _():
            for n in range(1, NT):
                from_owner(n).wait_send()

    for k in range(1, 9):
        for c in range(CHUNKS):
            take(ring_up, 0, k - 1, up[k] if k < 8 else z, c, k < 8)
            if k < 8:
                take(ring_down, 1, k - 1, down[k] if k < 7 else z, c, k < 7)
        for i in range(2 * k + 6, min(2 * k + 8, 16)):
            cross_over(i)
        for i in range(2 * k + 2, min(2 * k + 4, 16)):
            add_cores(i)
        if k == 1:
            pl.semaphore_wait(known_two, len(corners))
            pl.semaphore_wait(known_z.at[1], 2)
            tell(known_z.at[2], [along_z(4), along_z(-4)])
            early_copies = []
            for n in range(1, NT):
                early_copies.append(
                    send(
                        early.at[lax.rem(tensor + n, NT)], early_in.at[n],
                        early_send.at[n], early_recv.at[n], in_plane(n),
                    )
                )
        if k == 2:
            pl.semaphore_wait(known_z.at[2], 2)
            tell(known_z.at[3], [sibling])
        if k == 3:
            pl.semaphore_wait(known_z.at[3], 1)
            total = early[tensor]
            for n in range(1, NT):
                early_copies[n - 1].wait_recv()
                total = total + early_in[n]
            early_sum[...] = total
            for half in range(2):

                @pl.when(dp != 2 * tensor + half)
                def _():
                    to_owner(half).start()

                @pl.when(dp == 2 * tensor + half)
                def _():
                    plane_in[dp] = early_sum[half]
        if k == 6:

            @pl.when(z == tensor)
            def _():
                for source in range(2 * NZ):

                    @pl.when(dp != source)
                    def _():
                        pltpu.make_async_remote_copy(
                            src_ref=early_sum.at[0], dst_ref=plane_in.at[source], send_sem=plane_send.at[0],
                            recv_sem=plane_recv.at[source], device_id=sibling, device_id_type=MESH,
                        ).wait_recv()

                total = plane_in[0]
                for source in range(1, 2 * NZ):
                    total = total + plane_in[source]
                first[...] = total * (1.0 / 32.0)
                for n in range(1, NT):
                    from_owner(n).start()

    @pl.when(z != tensor)
    def _():
        from_owner(1).wait_recv()

    for part_ref, value in zip(mean_parts, split_three(own[z] * (1.0 / 32.0))):
        part_ref[0:block, :] = value

    def sum_in_plane(value):
        share[...] = value
        copies = []
        for k in range(1, NT):
            copies.append(
                send(
                    share, shares.at[tensor],
                    share_send.at[k], share_recv.at[k], in_plane(k),
                )
            )
        shares[tensor] = value
        return copies

    def plane_total(copies):
        for copy in copies:
            copy.wait_recv()
        total = shares[0]
        for k in range(1, NT):
            total = total + shares[k]
        return total

    group, place = z // 4, z % 4

    def sum_near(sweep, value):
        half = value.shape[0] // 2
        term[sweep, 0 : 2 * half, :] = value
        kept = pl.ds(0, half)
        swap = send(
            term.at[sweep, pl.ds(other * half, half)], pair.at[sweep, kept],
            pair_send.at[sweep], pair_recv.at[sweep], sibling,
        )
        swap.wait_recv()
        near[sweep, place, kept, :] = term[sweep, pl.ds(core * half, half), :] + pair[sweep, kept, :]
        copies = []
        for k in range(1, 4):
            device = ((group * 4 + (place + k) % 4) * 2 + core, tensor)
            copies.append(
                send(
                    near.at[sweep, place, kept], near.at[sweep, place, kept],
                    near_send.at[sweep, k], near_recv.at[sweep, k], device,
                )
            )
        for copy in copies:
            copy.wait_recv()
        far[sweep, group, kept, :] = (
            near[sweep, 0, kept, :] + near[sweep, 1, kept, :] + near[sweep, 2, kept, :] + near[sweep, 3, kept, :]
        )
        copies = []
        for k in (2, 1, 3):
            copies.append(
                send(
                    far.at[sweep, group, kept], far.at[sweep, group, kept],
                    far_send.at[sweep, k], far_recv.at[sweep, k], along_z(4 * k),
                )
            )
        return copies

    def sum_far(sweep, half, copies):
        kept = pl.ds(0, half)
        for copy in copies:
            copy.wait_recv()
        halves[sweep, core, kept, :] = (
            far[sweep, 0, kept, :] + far[sweep, 1, kept, :] + far[sweep, 2, kept, :] + far[sweep, 3, kept, :]
        )
        return send(
            halves.at[sweep, core, kept], halves.at[sweep, core, kept],
            half_send.at[sweep], half_recv.at[sweep], sibling,
        )

    pad = jnp.zeros((RANK, LANES - RANK), F32)

    def product(value, contract):
        stacked = jnp.concatenate(split_three(value), axis=0)
        dims = (((1,), (contract,)), ((), ()))
        by_top = lax.dot_general(stacked, mean_top[...], dims, preferred_element_type=F32)
        by_middle = lax.dot_general(stacked[: 2 * RANK], mean_middle[...], dims, preferred_element_type=F32)
        by_low = lax.dot_general(stacked[:RANK], mean_low[...], dims, preferred_element_type=F32)
        small = by_top[2 * RANK :] + by_middle[RANK:] + by_low
        return by_top[:RANK] + ((by_top[RANK : 2 * RANK] + by_middle[:RANK]) + small)

    left = first[...]
    wide = product(left, 0)
    gram = jnp.concatenate([dot_nt(left, left), pad], axis=1)
    value = jnp.concatenate([wide[:, :LANES], gram[:8], wide[:, LANES:], gram[8:]], axis=0)
    sum_far(0, RANK + 8, sum_near(0, value)).wait_recv()
    right = jnp.concatenate([halves[0, 0, 0:RANK, :], halves[0, 1, 0:RANK, :]], axis=1)
    copies = sum_in_plane(product(right, 1))
    gram = jnp.concatenate([halves[0, 0, RANK : RANK + 8, :], halves[0, 1, RANK : RANK + 8, :]], axis=0)
    inverse = inverse_factor(gram)

    left = dot_nn(inverse, plane_total(copies))
    behind = jnp.concatenate([jnp.zeros((block, LANES), F32), left, jnp.zeros((LANES - block - RANK, LANES), F32)], axis=0)
    gathered[dp] = left + dot_nt(left, behind)

    def relayed():
        return pltpu.make_async_remote_copy(
            src_ref=gathered.at[dp], dst_ref=relay, send_sem=relay_send, recv_sem=relay_recv,
            device_id=along_z(tensor), device_id_type=MESH,
        )

    @pl.when(tensor > 0)
    def _():
        relayed().start()

    def hand_done():
        @pl.when(tensor > 0)
        def _():
            for k in range(1, NT):
                handed(k).wait_send()

    passing = [send(gathered.at[dp], gathered.at[dp], pass_send.at[0], pass_recv.at[0], sibling)]
    wide = product(left, 0)
    far_copies = sum_near(1, jnp.concatenate([wide[:, :LANES], wide[:, LANES:]], axis=0))

    origin = lax.rem(z - tensor + NZ, NZ) * 2 + core

    def handed(k):
        return pltpu.make_async_remote_copy(
            src_ref=relay, dst_ref=gathered.at[origin], send_sem=gather_send.at[k],
            recv_sem=gather_recv.at[tensor], device_id=in_plane(k), device_id_type=MESH,
        )

    @pl.when(tensor > 0)
    def _():
        relayed().wait()
        for k in range(1, NT):
            handed(k).start()
        gathered[origin] = relay[...]

    def turn(index):
        top, middle, low = split_three(gathered[index])
        turned[index] = jnp.concatenate([top, middle, top, low, middle, top], axis=0).T

    turn(dp)
    for k in range(1, NT):
        source = lax.rem(z - k + NZ, NZ) * 2 + core

        @pl.when(tensor != k)
        def _():
            pltpu.make_async_remote_copy(
                src_ref=relay, dst_ref=gathered.at[source], send_sem=gather_send.at[k],
                recv_sem=gather_recv.at[k], device_id=in_plane(k), device_id_type=MESH,
            ).wait_recv()

        passing.append(
            send(gathered.at[source], gathered.at[source], pass_send.at[k], pass_recv.at[k], sibling)
        )
        turn(source)
    for k, copy in enumerate(passing):
        copy.wait_recv()
        turn(lax.rem(z - k + NZ, NZ) * 2 + other)
    gram = gathered[0]
    for d in range(1, 2 * NZ):
        gram = gram + gathered[d]
    inverse = inverse_factor(pltpu.roll(gram, LANES - block, 1))
    last = sum_far(1, RANK, far_copies)
    last.wait_recv()
    right = dot_nn(inverse, jnp.concatenate([halves[1, 0, 0:RANK, :], halves[1, 1, 0:RANK, :]], axis=1))
    right_ref[...] = right
    weights = lax.dot_general(inverse, right, (((0,), (0,)), ((), ())), precision=HIGH, preferred_element_type=F32)
    top, middle, low = split_three(weights)
    stacked = jnp.concatenate([top, top, middle, top, middle, low], axis=0)
    for d in range(2 * NZ):
        rows = pl.ds(d * block, block)
        approx = jnp.dot(turned[d], stacked, preferred_element_type=F32)
        total = g_ref[rows, :].astype(F32) + e_ref[rows, :].astype(F32)
        out_ref[0, rows, :] = (total - approx[:block]).astype(jnp.bfloat16)

    early_done()
    hand_done()
    for copy in sent:
        copy.wait_send()


def per_device(gradient, error_in, q_start):
    rows, columns = gradient.shape[1:]
    block = rows // (2 * NZ)
    hbm = pl.BlockSpec(memory_space=pltpu.HBM)
    vmem = pl.BlockSpec(memory_space=pltpu.VMEM)
    dma = pltpu.SemaphoreType.DMA
    half = RANK + 8
    return pl.pallas_call(
        compress,
        out_shape=[
            jax.ShapeDtypeStruct(gradient.shape, gradient.dtype),
            jax.ShapeDtypeStruct((RANK, columns), F32),
        ],
        in_specs=[hbm, hbm, hbm],
        out_specs=[vmem, vmem],
        scratch_shapes=[
            pltpu.VMEM((rows, columns), jnp.bfloat16),
            pltpu.VMEM((rows, columns), jnp.bfloat16),
            pltpu.VMEM((RANK, columns), F32),
            pltpu.VMEM((NT, 2, RANK, LANES), F32),
            pltpu.VMEM((NT, 2, RANK, LANES), F32),
            pltpu.VMEM((2, RANK, LANES), F32),
            pltpu.VMEM((2 * NZ, RANK, LANES), F32),
            pltpu.VMEM((RANK, LANES), F32),
            pltpu.VMEM((NZ, block, columns), F32),
            pltpu.VMEM((NZ, block, columns), F32),
            pltpu.VMEM((NZ, block, columns), F32),
            pltpu.VMEM((2, 8, block, columns), F32),
            pltpu.VMEM((LANES, columns), jnp.bfloat16),
            pltpu.VMEM((LANES, columns), jnp.bfloat16),
            pltpu.VMEM((LANES, columns), jnp.bfloat16),
            pltpu.VMEM((RANK, LANES), F32),
            pltpu.VMEM((NT, RANK, LANES), F32),
            pltpu.VMEM((2, 2 * half, LANES), F32),
            pltpu.VMEM((2, half, LANES), F32),
            pltpu.VMEM((2, 4, half, LANES), F32),
            pltpu.VMEM((2, 4, half, LANES), F32),
            pltpu.VMEM((2, 2, half, LANES), F32),
            pltpu.VMEM((RANK, LANES), F32),
            pltpu.VMEM((2 * NZ, RANK, LANES), F32),
            pltpu.VMEM((2 * NZ, LANES, 6 * RANK), jnp.bfloat16),
            dma((2, NZ)),
            dma((NZ,)), dma((NZ,)),
            dma((2, 8, CHUNKS)), dma((2, 8, CHUNKS)),
            dma((NT,)), dma((NT,)),
            dma((2,)), dma((2,)),
            dma((2, 4)), dma((2, 4)),
            dma((2, 4)), dma((2, 4)),
            dma((2,)), dma((2,)),
            dma((NT,)), dma((NT,)),
            dma((2,)), dma((2 * NZ,)),
            dma((NT,)), dma, dma,
            dma, dma,
            dma((NT,)), dma((NT,)),
            dma((NZ,)), dma((NZ,)),
            pltpu.SemaphoreType.REGULAR, pltpu.SemaphoreType.REGULAR, pltpu.SemaphoreType.REGULAR((4,)),
        ],
        compiler_params=pltpu.CompilerParams(
            collective_id=0, has_side_effects=True, vmem_limit_bytes=52 * 2**20
        ),
        name="compress",
    )(gradient, error_in, q_start)


def solution(mesh):
    placed = (P("dp", None, "tensor"), P("dp", None, "tensor"), P(None, "tensor"))
    return jax.shard_map(
        per_device,
        mesh=mesh,
        in_specs=placed,
        out_specs=(P("dp", None, "tensor"), P(None, "tensor")),
        check_vma=False,
    )
```

```python
import jax
import jax.numpy as jnp
from jax import lax
from jax.experimental import pallas as pl
from jax.experimental.pallas import tpu as pltpu
from jax.sharding import PartitionSpec as P

MESH = pl.DeviceIdType.MESH
F32 = jnp.float32
HIGH = lax.Precision.HIGHEST

RANK = 16
LANES = 128
NZ = 16
NT = 16
PIECES = 8
CHUNKS = 4


def dot_nn(a, b):
    return lax.dot_general(a, b, (((1,), (0,)), ((), ())), precision=HIGH, preferred_element_type=F32)


def dot_nt(a, b):
    return lax.dot_general(a, b, (((1,), (1,)), ((), ())), precision=HIGH, preferred_element_type=F32)


def inverse_factor(gram):
    rows = lax.broadcasted_iota(jnp.int32, (RANK, LANES), 0)
    lanes = lax.broadcasted_iota(jnp.int32, (RANK, LANES), 1)
    both = gram + (lanes == rows + RANK).astype(F32)
    for j in range(RANK):
        column = both[:, j : j + 1]
        scale = 1.0 / jnp.sqrt(column[j : j + 1, :])
        pivot = both[j : j + 1, :] * scale
        step = both - (column * scale) * pivot
        both = jnp.where(rows == j, pivot, jnp.where(rows > j, step, both))
    return both[:, RANK : 2 * RANK]


def split_three(value):
    top = value.astype(jnp.bfloat16)
    rest = value - top.astype(F32)
    middle = rest.astype(jnp.bfloat16)
    return top, middle, (rest - middle.astype(F32)).astype(jnp.bfloat16)


def compress(
    g_hbm, e_hbm, q_hbm, g_ref, e_ref, turned, stacked_ref, right_ref,
    q_ref, early, early_in, early_sum, plane_in, first, own, cross, cross_in, ring, mean_top, mean_middle, mean_low, share, shares, term, pair, near, far, halves, relay, gathered,
    load_sem, cross_send, cross_recv, ring_send, ring_recv, share_send, share_recv,
    pair_send, pair_recv, near_send, near_recv, far_send, far_recv, half_send, half_recv,
    early_send, early_recv, plane_send, plane_recv, owner_send, owner_recv, q_sem,
    relay_send, relay_recv, gather_send, gather_recv, pass_send, pass_recv, known_one, known_two, known_z,
):
    dp, tensor = lax.axis_index("dp"), lax.axis_index("tensor")
    z, core = dp // 2, dp % 2
    x, y = tensor // 4, tensor % 4
    mean_parts = (mean_top, mean_middle, mean_low)
    block = own.shape[1]
    other = 1 - core

    up = [lax.rem(z + 8 - k, NZ) for k in range(8)]
    down = [lax.rem(z + 9 + k, NZ) for k in range(7)]
    order = []
    for k in range(8):
        order.append(up[k])
        if k < 7:
            order.append(down[k])
    order.append(z)

    q_load = pltpu.make_async_copy(q_hbm, q_ref, q_sem)
    loads = []
    for i, j in enumerate(order):
        rows = pl.ds(pl.multiple_of(j * (2 * block), 2 * block), 2 * block)
        loads.append(
            (
                pltpu.make_async_copy(g_hbm.at[0, rows], g_ref.at[rows], load_sem.at[0, i]),
                pltpu.make_async_copy(e_hbm.at[0, rows], e_ref.at[rows], load_sem.at[1, i]),
            )
        )
        for load in loads[i]:
            load.start()
        if i == 1:
            q_load.start()

    sibling = (z * 2 + other, tensor)

    def along_z(hops):
        return (lax.rem(z + hops + NZ, NZ) * 2 + core, tensor)

    def in_plane(k):
        return (dp, lax.rem(tensor + k, NT))

    def hop(dx, dy):
        return (dp, lax.rem(x + dx + 4, 4) * 4 + lax.rem(y + dy + 4, 4))

    steps = [hop(1, 0), hop(-1, 0), hop(0, 1), hop(0, -1)]
    neighbours = [sibling, along_z(1), along_z(-1)] + steps
    barrier = pltpu.get_barrier_semaphore()
    for device in neighbours:
        pl.semaphore_signal(barrier, inc=1, device_id=device, device_id_type=MESH)
    for part_ref in mean_parts:
        part_ref[...] = jnp.zeros_like(part_ref)
    early[...] = jnp.zeros_like(early)
    early_sum[...] = jnp.zeros_like(early_sum)

    def accumulated(index):
        rows = pl.ds(pl.multiple_of(index * block, block), block)
        return g_ref[rows, :].astype(F32) + e_ref[rows, :].astype(F32)

    def wait_load(i):
        for load in loads[i]:
            load.wait()

    for i in range(4):
        wait_load(i)
        cross[i] = accumulated(2 * order[i] + other)
    pl.semaphore_wait(barrier, len(neighbours))

    def tell(semaphore, devices):
        for device in devices:
            pl.semaphore_signal(semaphore, inc=1, device_id=device, device_id_type=MESH)

    corners = [hop(2, 0), hop(0, 2), hop(1, 1), hop(1, -1), hop(-1, 1), hop(-1, -1)]
    tell(known_one, steps)
    tell(known_z.at[0], [along_z(1), along_z(-1)])

    sent = []

    def send(src, dst, send_sem, recv_sem, device):
        copy = pltpu.make_async_remote_copy(
            src_ref=src, dst_ref=dst, send_sem=send_sem, recv_sem=recv_sem, device_id=device, device_id_type=MESH
        )
        copy.start()
        sent.append(copy)
        return copy

    part = block // CHUNKS

    def forward(direction, k, target, c):
        rows = pl.ds(c * part, part)
        return send(
            own.at[target, rows], ring.at[direction, k, rows],
            ring_send.at[direction, k, c], ring_recv.at[direction, k, c],
            along_z(1 if direction == 0 else -1),
        )

    crossing = []

    def cross_over(i):
        if i >= 4:
            cross[i] = accumulated(2 * order[i] + other)
        crossing.append(send(cross.at[i], cross_in.at[i], cross_send.at[i], cross_recv.at[i], sibling))

    def add_cores(i):
        mine = accumulated(2 * order[i] + core)
        crossing[i].wait_recv()
        own[order[i]] = mine + cross_in[i]

    for i in range(4):
        cross_over(i)
    q_load.wait()
    q_parts = jnp.concatenate(split_three(q_ref[...]), axis=0)

    def early_term(j):
        for half in range(2):
            rows = pl.ds(pl.multiple_of((2 * j + half) * block, block), block)
            dims = (((1,), (1,)), ((), ()))
            three = lax.dot_general(q_parts, g_ref[rows, :], dims, preferred_element_type=F32)
            three = three + lax.dot_general(q_parts, e_ref[rows, :], dims, preferred_element_type=F32)
            early[j, half, :, 0:block] = three[:RANK] + (three[RANK : 2 * RANK] + three[2 * RANK :])

    for i in range(0, 4):
        early_term(order[i])
    add_cores(0)
    ring_up = [forward(0, 0, up[0], c) for c in range(CHUNKS)]
    add_cores(1)
    ring_down = [forward(1, 0, down[0], c) for c in range(CHUNKS)]
    for i in range(4, 8):
        wait_load(i)
        cross_over(i)
    for i in range(8, 16):
        wait_load(i)
    for i in range(4, 16):
        early_term(order[i])
    add_cores(2)
    add_cores(3)
    pl.semaphore_wait(known_one, len(steps))
    pl.semaphore_wait(known_z.at[0], 2)
    tell(known_two, corners)
    tell(known_z.at[1], [along_z(2), along_z(-2)])

    def take(copies, direction, k, target, c, onward):
        rows = pl.ds(c * part, part)
        copies[c].wait_recv()
        own[target, rows, :] = own[target, rows, :] + ring[direction, k, rows, :]
        if onward:
            copies[c] = forward(direction, k + 1, target, c)

    def to_owner(half):
        return pltpu.make_async_remote_copy(
            src_ref=early_sum.at[half], dst_ref=plane_in.at[dp], send_sem=plane_send.at[half],
            recv_sem=plane_recv.at[dp], device_id=(2 * tensor + half, tensor), device_id_type=MESH,
        )

    def from_owner(n):
        return pltpu.make_async_remote_copy(
            src_ref=first, dst_ref=first, send_sem=owner_send.at[n], recv_sem=owner_recv,
            device_id=in_plane(n), device_id_type=MESH,
        )

    def early_done():
        for half in range(2):

            @pl.when(dp != 2 * tensor + half)
            def _():
                to_owner(half).wait_send()

        @pl.when(z == tensor)
        def _():
            for n in range(1, NT):
                from_owner(n).wait_send()

    for k in range(1, 9):
        for c in range(CHUNKS):
            take(ring_up, 0, k - 1, up[k] if k < 8 else z, c, k < 8)
            if k < 8:
                take(ring_down, 1, k - 1, down[k] if k < 7 else z, c, k < 7)
        for i in range(2 * k + 6, min(2 * k + 8, 16)):
            cross_over(i)
        for i in range(2 * k + 2, min(2 * k + 4, 16)):
            add_cores(i)
        if k == 1:
            pl.semaphore_wait(known_two, len(corners))
            pl.semaphore_wait(known_z.at[1], 2)
            tell(known_z.at[2], [along_z(4), along_z(-4)])
            early_copies = []
            for n in range(1, NT):
                early_copies.append(
                    send(
                        early.at[lax.rem(tensor + n, NT)], early_in.at[n],
                        early_send.at[n], early_recv.at[n], in_plane(n),
                    )
                )
        if k == 2:
            pl.semaphore_wait(known_z.at[2], 2)
            tell(known_z.at[3], [sibling])
        if k == 3:
            pl.semaphore_wait(known_z.at[3], 1)
            total = early[tensor]
            for n in range(1, NT):
                early_copies[n - 1].wait_recv()
                total = total + early_in[n]
            early_sum[...] = total
            for half in range(2):

                @pl.when(dp != 2 * tensor + half)
                def _():
                    to_owner(half).start()

                @pl.when(dp == 2 * tensor + half)
                def _():
                    plane_in[dp] = early_sum[half]
        if k == 6:

            @pl.when(z == tensor)
            def _():
                for source in range(2 * NZ):

                    @pl.when(dp != source)
                    def _():
                        pltpu.make_async_remote_copy(
                            src_ref=early_sum.at[0], dst_ref=plane_in.at[source], send_sem=plane_send.at[0],
                            recv_sem=plane_recv.at[source], device_id=sibling, device_id_type=MESH,
                        ).wait_recv()

                total = plane_in[0]
                for source in range(1, 2 * NZ):
                    total = total + plane_in[source]
                first[...] = total * (1.0 / 32.0)
                for n in range(1, NT):
                    from_owner(n).start()

    @pl.when(z != tensor)
    def _():
        from_owner(1).wait_recv()

    for part_ref, value in zip(mean_parts, split_three(own[z] * (1.0 / 32.0))):
        part_ref[0:block, :] = value

    def sum_in_plane(value):
        share[...] = value
        copies = []
        for k in range(1, NT):
            copies.append(
                send(
                    share, shares.at[tensor],
                    share_send.at[k], share_recv.at[k], in_plane(k),
                )
            )
        shares[tensor] = value
        return copies

    def plane_total(copies):
        for copy in copies:
            copy.wait_recv()
        total = shares[0]
        for k in range(1, NT):
            total = total + shares[k]
        return total

    group, place = z // 4, z % 4

    def sum_near(sweep, value):
        half = value.shape[0] // 2
        term[sweep, 0 : 2 * half, :] = value
        kept = pl.ds(0, half)
        swap = send(
            term.at[sweep, pl.ds(other * half, half)], pair.at[sweep, kept],
            pair_send.at[sweep], pair_recv.at[sweep], sibling,
        )
        swap.wait_recv()
        near[sweep, place, kept, :] = term[sweep, pl.ds(core * half, half), :] + pair[sweep, kept, :]
        copies = []
        for k in range(1, 4):
            device = ((group * 4 + (place + k) % 4) * 2 + core, tensor)
            copies.append(
                send(
                    near.at[sweep, place, kept], near.at[sweep, place, kept],
                    near_send.at[sweep, k], near_recv.at[sweep, k], device,
                )
            )
        for copy in copies:
            copy.wait_recv()
        far[sweep, group, kept, :] = (
            near[sweep, 0, kept, :] + near[sweep, 1, kept, :] + near[sweep, 2, kept, :] + near[sweep, 3, kept, :]
        )
        copies = []
        for k in (2, 1, 3):
            copies.append(
                send(
                    far.at[sweep, group, kept], far.at[sweep, group, kept],
                    far_send.at[sweep, k], far_recv.at[sweep, k], along_z(4 * k),
                )
            )
        return copies

    def sum_far(sweep, half, copies):
        kept = pl.ds(0, half)
        for copy in copies:
            copy.wait_recv()
        halves[sweep, core, kept, :] = (
            far[sweep, 0, kept, :] + far[sweep, 1, kept, :] + far[sweep, 2, kept, :] + far[sweep, 3, kept, :]
        )
        return send(
            halves.at[sweep, core, kept], halves.at[sweep, core, kept],
            half_send.at[sweep], half_recv.at[sweep], sibling,
        )

    pad = jnp.zeros((RANK, LANES - RANK), F32)

    def product(value, contract):
        stacked = jnp.concatenate(split_three(value), axis=0)
        dims = (((1,), (contract,)), ((), ()))
        by_top = lax.dot_general(stacked, mean_top[...], dims, preferred_element_type=F32)
        by_middle = lax.dot_general(stacked[: 2 * RANK], mean_middle[...], dims, preferred_element_type=F32)
        by_low = lax.dot_general(stacked[:RANK], mean_low[...], dims, preferred_element_type=F32)
        small = by_top[2 * RANK :] + by_middle[RANK:] + by_low
        return by_top[:RANK] + ((by_top[RANK : 2 * RANK] + by_middle[:RANK]) + small)

    left = first[...]
    wide = product(left, 0)
    gram = jnp.concatenate([dot_nt(left, left), pad], axis=1)
    value = jnp.concatenate([wide[:, :LANES], gram[:8], wide[:, LANES:], gram[8:]], axis=0)
    sum_far(0, RANK + 8, sum_near(0, value)).wait_recv()
    right = jnp.concatenate([halves[0, 0, 0:RANK, :], halves[0, 1, 0:RANK, :]], axis=1)
    copies = sum_in_plane(product(right, 1))
    gram = jnp.concatenate([halves[0, 0, RANK : RANK + 8, :], halves[0, 1, RANK : RANK + 8, :]], axis=0)
    inverse = inverse_factor(gram)

    left = dot_nn(inverse, plane_total(copies))
    behind = jnp.concatenate([jnp.zeros((block, LANES), F32), left, jnp.zeros((LANES - block - RANK, LANES), F32)], axis=0)
    gathered[dp] = left + dot_nt(left, behind)

    def relayed():
        return pltpu.make_async_remote_copy(
            src_ref=gathered.at[dp], dst_ref=relay, send_sem=relay_send, recv_sem=relay_recv,
            device_id=along_z(tensor), device_id_type=MESH,
        )

    @pl.when(tensor > 0)
    def _():
        relayed().start()

    def hand_done():
        @pl.when(tensor > 0)
        def _():
            for k in range(1, NT):
                handed(k).wait_send()

    passing = [send(gathered.at[dp], gathered.at[dp], pass_send.at[0], pass_recv.at[0], sibling)]
    wide = product(left, 0)
    far_copies = sum_near(1, jnp.concatenate([wide[:, :LANES], wide[:, LANES:]], axis=0))

    origin = lax.rem(z - tensor + NZ, NZ) * 2 + core

    def handed(k):
        return pltpu.make_async_remote_copy(
            src_ref=relay, dst_ref=gathered.at[origin], send_sem=gather_send.at[k],
            recv_sem=gather_recv.at[tensor], device_id=in_plane(k), device_id_type=MESH,
        )

    @pl.when(tensor > 0)
    def _():
        relayed().wait()
        for k in range(1, NT):
            handed(k).start()
        gathered[origin] = relay[...]

    def turn(index):
        top, middle, low = split_three(gathered[index])
        turned[index] = jnp.concatenate([top, middle, top, low, middle, top], axis=0).T

    turn(dp)
    for k in range(1, NT):
        source = lax.rem(z - k + NZ, NZ) * 2 + core

        @pl.when(tensor != k)
        def _():
            pltpu.make_async_remote_copy(
                src_ref=relay, dst_ref=gathered.at[source], send_sem=gather_send.at[k],
                recv_sem=gather_recv.at[k], device_id=in_plane(k), device_id_type=MESH,
            ).wait_recv()

        passing.append(
            send(gathered.at[source], gathered.at[source], pass_send.at[k], pass_recv.at[k], sibling)
        )
        turn(source)
    for k, copy in enumerate(passing):
        copy.wait_recv()
        turn(lax.rem(z - k + NZ, NZ) * 2 + other)
    gram = gathered[0]
    for d in range(1, 2 * NZ):
        gram = gram + gathered[d]
    inverse = inverse_factor(pltpu.roll(gram, LANES - block, 1))
    last = sum_far(1, RANK, far_copies)
    last.wait_recv()
    right = dot_nn(inverse, jnp.concatenate([halves[1, 0, 0:RANK, :], halves[1, 1, 0:RANK, :]], axis=1))
    right_ref[...] = right
    weights = lax.dot_general(inverse, right, (((0,), (0,)), ((), ())), precision=HIGH, preferred_element_type=F32)
    top, middle, low = split_three(weights)
    stacked_ref[...] = jnp.concatenate([top, top, middle, top, middle, low], axis=0)
    early_done()
    hand_done()
    for copy in sent:
        copy.wait_send()


def residual(g_ref, e_ref, turned, stacked_ref, right_ref, out_hbm, right_hbm, out_ref, out_sem, right_sem):
    blocks = turned.shape[0]
    block = out_ref.shape[0] // blocks
    copies = [pltpu.make_async_copy(right_ref, right_hbm, right_sem)]
    copies[0].start()
    each = blocks // PIECES
    for piece in range(PIECES):
        for d in range(piece * each, (piece + 1) * each):
            rows = pl.ds(d * block, block)
            approx = jnp.dot(turned[d], stacked_ref[...], preferred_element_type=F32)
            total = g_ref[rows, :].astype(F32) + e_ref[rows, :].astype(F32)
            out_ref[rows, :] = (total - approx[:block]).astype(jnp.bfloat16)
        rows = pl.ds(piece * each * block, each * block)
        copies.append(pltpu.make_async_copy(out_ref.at[rows], out_hbm.at[0, rows], out_sem.at[piece]))
        copies[-1].start()
    for copy in copies:
        copy.wait()


def per_device(gradient, error_in, q_start):
    rows, columns = gradient.shape[1:]
    block = rows // (2 * NZ)
    hbm = pl.BlockSpec(memory_space=pltpu.HBM)
    vmem = pl.BlockSpec(memory_space=pltpu.VMEM)
    dma = pltpu.SemaphoreType.DMA
    half = RANK + 8
    kept = pl.pallas_call(
        compress,
        out_shape=[
            jax.ShapeDtypeStruct((rows, columns), jnp.bfloat16),
            jax.ShapeDtypeStruct((rows, columns), jnp.bfloat16),
            jax.ShapeDtypeStruct((2 * NZ, LANES, 6 * RANK), jnp.bfloat16),
            jax.ShapeDtypeStruct((6 * RANK, columns), jnp.bfloat16),
            jax.ShapeDtypeStruct((RANK, columns), F32),
        ],
        in_specs=[hbm, hbm, hbm],
        out_specs=[vmem] * 5,
        scratch_shapes=[
            pltpu.VMEM((RANK, columns), F32),
            pltpu.VMEM((NT, 2, RANK, LANES), F32),
            pltpu.VMEM((NT, 2, RANK, LANES), F32),
            pltpu.VMEM((2, RANK, LANES), F32),
            pltpu.VMEM((2 * NZ, RANK, LANES), F32),
            pltpu.VMEM((RANK, LANES), F32),
            pltpu.VMEM((NZ, block, columns), F32),
            pltpu.VMEM((NZ, block, columns), F32),
            pltpu.VMEM((NZ, block, columns), F32),
            pltpu.VMEM((2, 8, block, columns), F32),
            pltpu.VMEM((LANES, columns), jnp.bfloat16),
            pltpu.VMEM((LANES, columns), jnp.bfloat16),
            pltpu.VMEM((LANES, columns), jnp.bfloat16),
            pltpu.VMEM((RANK, LANES), F32),
            pltpu.VMEM((NT, RANK, LANES), F32),
            pltpu.VMEM((2, 2 * half, LANES), F32),
            pltpu.VMEM((2, half, LANES), F32),
            pltpu.VMEM((2, 4, half, LANES), F32),
            pltpu.VMEM((2, 4, half, LANES), F32),
            pltpu.VMEM((2, 2, half, LANES), F32),
            pltpu.VMEM((RANK, LANES), F32),
            pltpu.VMEM((2 * NZ, RANK, LANES), F32),
            dma((2, NZ)),
            dma((NZ,)), dma((NZ,)),
            dma((2, 8, CHUNKS)), dma((2, 8, CHUNKS)),
            dma((NT,)), dma((NT,)),
            dma((2,)), dma((2,)),
            dma((2, 4)), dma((2, 4)),
            dma((2, 4)), dma((2, 4)),
            dma((2,)), dma((2,)),
            dma((NT,)), dma((NT,)),
            dma((2,)), dma((2 * NZ,)),
            dma((NT,)), dma, dma,
            dma, dma,
            dma((NT,)), dma((NT,)),
            dma((NZ,)), dma((NZ,)),
            pltpu.SemaphoreType.REGULAR, pltpu.SemaphoreType.REGULAR, pltpu.SemaphoreType.REGULAR((4,)),
        ],
        compiler_params=pltpu.CompilerParams(
            collective_id=0, has_side_effects=True, vmem_limit_bytes=49 * 2**20 + 2**18
        ),
        name="compress",
    )(gradient, error_in, q_start)
    return pl.pallas_call(
        residual,
        out_shape=[
            jax.ShapeDtypeStruct(gradient.shape, gradient.dtype),
            jax.ShapeDtypeStruct((RANK, columns), F32),
        ],
        in_specs=[vmem] * 5,
        out_specs=[hbm, hbm],
        scratch_shapes=[pltpu.VMEM((rows, columns), jnp.bfloat16), dma((PIECES,)), dma],
        compiler_params=pltpu.CompilerParams(vmem_limit_bytes=16 * 2**20),
        name="residual",
    )(*kept)


def solution(mesh):
    placed = (P("dp", None, "tensor"), P("dp", None, "tensor"), P(None, "tensor"))
    return jax.shard_map(
        per_device,
        mesh=mesh,
        in_specs=placed,
        out_specs=(P("dp", None, "tensor"), P(None, "tensor")),
        check_vma=False,
    )
```

```python
import jax
import jax.numpy as jnp
from jax import lax
from jax.experimental import pallas as pl
from jax.experimental.pallas import tpu as pltpu
from jax.sharding import PartitionSpec as P

MESH = pl.DeviceIdType.MESH
F32 = jnp.float32
HIGH = lax.Precision.HIGHEST

RANK = 16
LANES = 128
NZ = 16
NT = 16
PIECES = 8
CHUNKS = 4


def dot_nn(a, b):
    return lax.dot_general(a, b, (((1,), (0,)), ((), ())), precision=HIGH, preferred_element_type=F32)


def dot_nt(a, b):
    return lax.dot_general(a, b, (((1,), (1,)), ((), ())), precision=HIGH, preferred_element_type=F32)


def inverse_factor(gram):
    rows = lax.broadcasted_iota(jnp.int32, (RANK, LANES), 0)
    lanes = lax.broadcasted_iota(jnp.int32, (RANK, LANES), 1)
    both = gram + (lanes == rows + RANK).astype(F32)
    for j in range(RANK):
        column = both[:, j : j + 1]
        scale = 1.0 / jnp.sqrt(column[j : j + 1, :])
        pivot = both[j : j + 1, :] * scale
        step = both - (column * scale) * pivot
        both = jnp.where(rows == j, pivot, jnp.where(rows > j, step, both))
    return both[:, RANK : 2 * RANK]


def split_three(value):
    top = value.astype(jnp.bfloat16)
    rest = value - top.astype(F32)
    middle = rest.astype(jnp.bfloat16)
    return top, middle, (rest - middle.astype(F32)).astype(jnp.bfloat16)


def compress(
    g_hbm, e_hbm, q_hbm, g_ref, e_ref, turned, stacked_ref, right_ref,
    q_ref, early, early_in, early_sum, plane_in, first, own, cross, cross_in, ring, mean_top, mean_middle, mean_low, share, shares, term, pair, near, far, halves, relay, gathered,
    load_sem, cross_send, cross_recv, ring_send, ring_recv, share_send, share_recv,
    pair_send, pair_recv, near_send, near_recv, far_send, far_recv, half_send, half_recv,
    early_send, early_recv, plane_send, plane_recv, owner_send, owner_recv, q_sem,
    relay_send, relay_recv, gather_send, gather_recv, pass_send, pass_recv, known_one, known_two, known_z,
):
    dp, tensor = lax.axis_index("dp"), lax.axis_index("tensor")
    z, core = dp // 2, dp % 2
    x, y = tensor // 4, tensor % 4
    mean_parts = (mean_top, mean_middle, mean_low)
    block = own.shape[1]
    other = 1 - core

    up = [lax.rem(z + 8 - k, NZ) for k in range(8)]
    down = [lax.rem(z + 9 + k, NZ) for k in range(7)]
    order = []
    for k in range(8):
        order.append(up[k])
        if k < 7:
            order.append(down[k])
    order.append(z)

    q_load = pltpu.make_async_copy(q_hbm, q_ref, q_sem)
    loads = []
    for i, j in enumerate(order):
        rows = pl.ds(pl.multiple_of(j * (2 * block), 2 * block), 2 * block)
        loads.append(
            (
                pltpu.make_async_copy(g_hbm.at[0, rows], g_ref.at[rows], load_sem.at[0, i]),
                pltpu.make_async_copy(e_hbm.at[0, rows], e_ref.at[rows], load_sem.at[1, i]),
            )
        )
        for load in loads[i]:
            load.start()
        if i == 1:
            q_load.start()

    sibling = (z * 2 + other, tensor)

    def along_z(hops):
        return (lax.rem(z + hops + NZ, NZ) * 2 + core, tensor)

    def in_plane(k):
        return (dp, lax.rem(tensor + k, NT))

    def hop(dx, dy):
        return (dp, lax.rem(x + dx + 4, 4) * 4 + lax.rem(y + dy + 4, 4))

    steps = [hop(1, 0), hop(-1, 0), hop(0, 1), hop(0, -1)]
    neighbours = [sibling, along_z(1), along_z(-1)] + steps
    barrier = pltpu.get_barrier_semaphore()
    for device in neighbours:
        pl.semaphore_signal(barrier, inc=1, device_id=device, device_id_type=MESH)
    for part_ref in mean_parts:
        part_ref[...] = jnp.zeros_like(part_ref)
    early[...] = jnp.zeros_like(early)
    early_sum[...] = jnp.zeros_like(early_sum)

    def accumulated(index):
        rows = pl.ds(pl.multiple_of(index * block, block), block)
        return g_ref[rows, :].astype(F32) + e_ref[rows, :].astype(F32)

    def wait_load(i):
        for load in loads[i]:
            load.wait()

    for i in range(4):
        wait_load(i)
        cross[i] = accumulated(2 * order[i] + other)
    pl.semaphore_wait(barrier, len(neighbours))

    def tell(semaphore, devices):
        for device in devices:
            pl.semaphore_signal(semaphore, inc=1, device_id=device, device_id_type=MESH)

    corners = [hop(2, 0), hop(0, 2), hop(1, 1), hop(1, -1), hop(-1, 1), hop(-1, -1)]
    tell(known_one, steps)
    tell(known_z.at[0], [along_z(1), along_z(-1)])

    sent = []

    def send(src, dst, send_sem, recv_sem, device):
        copy = pltpu.make_async_remote_copy(
            src_ref=src, dst_ref=dst, send_sem=send_sem, recv_sem=recv_sem, device_id=device, device_id_type=MESH
        )
        copy.start()
        sent.append(copy)
        return copy

    part = block // CHUNKS

    def forward(direction, k, target, c):
        rows = pl.ds(c * part, part)
        return send(
            own.at[target, rows], ring.at[direction, k, rows],
            ring_send.at[direction, k, c], ring_recv.at[direction, k, c],
            along_z(1 if direction == 0 else -1),
        )

    crossing = []

    def cross_over(i):
        if i >= 4:
            cross[i] = accumulated(2 * order[i] + other)
        crossing.append(send(cross.at[i], cross_in.at[i], cross_send.at[i], cross_recv.at[i], sibling))

    def add_cores(i):
        mine = accumulated(2 * order[i] + core)
        crossing[i].wait_recv()
        own[order[i]] = mine + cross_in[i]

    for i in range(4):
        cross_over(i)
    q_load.wait()
    q_parts = jnp.concatenate(split_three(q_ref[...]), axis=0)

    def early_term(j):
        for half in range(2):
            rows = pl.ds(pl.multiple_of((2 * j + half) * block, block), block)
            dims = (((1,), (1,)), ((), ()))
            three = lax.dot_general(q_parts, g_ref[rows, :], dims, preferred_element_type=F32)
            three = three + lax.dot_general(q_parts, e_ref[rows, :], dims, preferred_element_type=F32)
            early[j, half, :, 0:block] = three[:RANK] + (three[RANK : 2 * RANK] + three[2 * RANK :])

    for i in range(0, 4):
        early_term(order[i])
    add_cores(0)
    ring_up = [forward(0, 0, up[0], c) for c in range(CHUNKS)]
    add_cores(1)
    ring_down = [forward(1, 0, down[0], c) for c in range(CHUNKS)]
    for i in range(4, 8):
        wait_load(i)
        cross_over(i)
    for i in range(8, 16):
        wait_load(i)
    for i in range(4, 16):
        early_term(order[i])
    add_cores(2)
    add_cores(3)
    pl.semaphore_wait(known_one, len(steps))
    pl.semaphore_wait(known_z.at[0], 2)
    tell(known_two, corners)
    tell(known_z.at[1], [along_z(2), along_z(-2)])

    def take(copies, direction, k, target, c, onward):
        rows = pl.ds(c * part, part)
        copies[c].wait_recv()
        own[target, rows, :] = own[target, rows, :] + ring[direction, k, rows, :]
        if onward:
            copies[c] = forward(direction, k + 1, target, c)

    def to_owner(half):
        return pltpu.make_async_remote_copy(
            src_ref=early_sum.at[half], dst_ref=plane_in.at[dp], send_sem=plane_send.at[half],
            recv_sem=plane_recv.at[dp], device_id=(2 * tensor + half, tensor), device_id_type=MESH,
        )

    def from_owner(n):
        return pltpu.make_async_remote_copy(
            src_ref=first, dst_ref=first, send_sem=owner_send.at[n], recv_sem=owner_recv,
            device_id=in_plane(n), device_id_type=MESH,
        )

    def early_done():
        for half in range(2):

            @pl.when(dp != 2 * tensor + half)
            def _():
                to_owner(half).wait_send()

        @pl.when(z == tensor)
        def _():
            for n in range(1, NT):
                from_owner(n).wait_send()

    for k in range(1, 9):
        for c in range(CHUNKS):
            take(ring_up, 0, k - 1, up[k] if k < 8 else z, c, k < 8)
            if k < 8:
                take(ring_down, 1, k - 1, down[k] if k < 7 else z, c, k < 7)
        for i in range(2 * k + 6, min(2 * k + 8, 16)):
            cross_over(i)
        for i in range(2 * k + 2, min(2 * k + 4, 16)):
            add_cores(i)
        if k == 1:
            pl.semaphore_wait(known_two, len(corners))
            pl.semaphore_wait(known_z.at[1], 2)
            tell(known_z.at[2], [along_z(4), along_z(-4)])
            early_copies = []
            for n in range(1, NT):
                early_copies.append(
                    send(
                        early.at[lax.rem(tensor + n, NT)], early_in.at[n],
                        early_send.at[n], early_recv.at[n], in_plane(n),
                    )
                )
        if k == 2:
            pl.semaphore_wait(known_z.at[2], 2)
            tell(known_z.at[3], [sibling])
        if k == 3:
            pl.semaphore_wait(known_z.at[3], 1)
            total = early[tensor]
            for n in range(1, NT):
                early_copies[n - 1].wait_recv()
                total = total + early_in[n]
            early_sum[...] = total
            for half in range(2):

                @pl.when(dp != 2 * tensor + half)
                def _():
                    to_owner(half).start()

                @pl.when(dp == 2 * tensor + half)
                def _():
                    plane_in[dp] = early_sum[half]
        if k == 6:

            @pl.when(z == tensor)
            def _():
                for source in range(2 * NZ):

                    @pl.when(dp != source)
                    def _():
                        pltpu.make_async_remote_copy(
                            src_ref=early_sum.at[0], dst_ref=plane_in.at[source], send_sem=plane_send.at[0],
                            recv_sem=plane_recv.at[source], device_id=sibling, device_id_type=MESH,
                        ).wait_recv()

                total = plane_in[0]
                for source in range(1, 2 * NZ):
                    total = total + plane_in[source]
                first[...] = total * (1.0 / 32.0)
                for n in range(1, NT):
                    from_owner(n).start()

    @pl.when(z != tensor)
    def _():
        from_owner(1).wait_recv()

    for part_ref, value in zip(mean_parts, split_three(own[z] * (1.0 / 32.0))):
        part_ref[0:block, :] = value

    def sum_in_plane(value):
        share[...] = value
        copies = []
        for k in range(1, NT):
            copies.append(
                send(
                    share, shares.at[tensor],
                    share_send.at[k], share_recv.at[k], in_plane(k),
                )
            )
        shares[tensor] = value
        return copies

    def plane_total(copies):
        for copy in copies:
            copy.wait_recv()
        total = shares[0]
        for k in range(1, NT):
            total = total + shares[k]
        return total

    group, place = z // 4, z % 4

    def sum_near(sweep, value):
        half = value.shape[0] // 2
        term[sweep, 0 : 2 * half, :] = value
        kept = pl.ds(0, half)
        swap = send(
            term.at[sweep, pl.ds(other * half, half)], pair.at[sweep, kept],
            pair_send.at[sweep], pair_recv.at[sweep], sibling,
        )
        swap.wait_recv()
        near[sweep, place, kept, :] = term[sweep, pl.ds(core * half, half), :] + pair[sweep, kept, :]
        copies = []
        for k in range(1, 4):
            device = ((group * 4 + (place + k) % 4) * 2 + core, tensor)
            copies.append(
                send(
                    near.at[sweep, place, kept], near.at[sweep, place, kept],
                    near_send.at[sweep, k], near_recv.at[sweep, k], device,
                )
            )
        for copy in copies:
            copy.wait_recv()
        far[sweep, group, kept, :] = (
            near[sweep, 0, kept, :] + near[sweep, 1, kept, :] + near[sweep, 2, kept, :] + near[sweep, 3, kept, :]
        )
        copies = []
        for k in (2, 1, 3):
            copies.append(
                send(
                    far.at[sweep, group, kept], far.at[sweep, group, kept],
                    far_send.at[sweep, k], far_recv.at[sweep, k], along_z(4 * k),
                )
            )
        return copies

    def sum_far(sweep, half, copies):
        kept = pl.ds(0, half)
        for copy in copies:
            copy.wait_recv()
        halves[sweep, core, kept, :] = (
            far[sweep, 0, kept, :] + far[sweep, 1, kept, :] + far[sweep, 2, kept, :] + far[sweep, 3, kept, :]
        )
        return send(
            halves.at[sweep, core, kept], halves.at[sweep, core, kept],
            half_send.at[sweep], half_recv.at[sweep], sibling,
        )

    pad = jnp.zeros((RANK, LANES - RANK), F32)

    def product(value, contract):
        stacked = jnp.concatenate(split_three(value), axis=0)
        dims = (((1,), (contract,)), ((), ()))
        by_top = lax.dot_general(stacked, mean_top[...], dims, preferred_element_type=F32)
        by_middle = lax.dot_general(stacked[: 2 * RANK], mean_middle[...], dims, preferred_element_type=F32)
        by_low = lax.dot_general(stacked[:RANK], mean_low[...], dims, preferred_element_type=F32)
        small = by_top[2 * RANK :] + by_middle[RANK:] + by_low
        return by_top[:RANK] + ((by_top[RANK : 2 * RANK] + by_middle[:RANK]) + small)

    left = first[...]
    wide = product(left, 0)
    gram = jnp.concatenate([dot_nt(left, left), pad], axis=1)
    value = jnp.concatenate([wide[:, :LANES], gram[:8], wide[:, LANES:], gram[8:]], axis=0)
    sum_far(0, RANK + 8, sum_near(0, value)).wait_recv()
    right = jnp.concatenate([halves[0, 0, 0:RANK, :], halves[0, 1, 0:RANK, :]], axis=1)
    copies = sum_in_plane(product(right, 1))
    gram = jnp.concatenate([halves[0, 0, RANK : RANK + 8, :], halves[0, 1, RANK : RANK + 8, :]], axis=0)
    inverse = inverse_factor(gram)

    left = dot_nn(inverse, plane_total(copies))
    behind = jnp.concatenate([jnp.zeros((block, LANES), F32), left, jnp.zeros((LANES - block - RANK, LANES), F32)], axis=0)
    gathered[dp] = left + dot_nt(left, behind)

    def relayed():
        return pltpu.make_async_remote_copy(
            src_ref=gathered.at[dp], dst_ref=relay, send_sem=relay_send, recv_sem=relay_recv,
            device_id=along_z(tensor), device_id_type=MESH,
        )

    @pl.when(tensor > 0)
    def _():
        relayed().start()

    def hand_done():
        @pl.when(tensor > 0)
        def _():
            for k in range(1, NT):
                handed(k).wait_send()

    passing = [send(gathered.at[dp], gathered.at[dp], pass_send.at[0], pass_recv.at[0], sibling)]
    wide = product(left, 0)
    far_copies = sum_near(1, jnp.concatenate([wide[:, :LANES], wide[:, LANES:]], axis=0))

    origin = lax.rem(z - tensor + NZ, NZ) * 2 + core

    def handed(k):
        return pltpu.make_async_remote_copy(
            src_ref=relay, dst_ref=gathered.at[origin], send_sem=gather_send.at[k],
            recv_sem=gather_recv.at[tensor], device_id=in_plane(k), device_id_type=MESH,
        )

    @pl.when(tensor > 0)
    def _():
        relayed().wait()
        for k in range(1, NT):
            handed(k).start()
        gathered[origin] = relay[...]

    def turn(index):
        top, middle, low = split_three(gathered[index])
        turned[index] = jnp.concatenate([top, middle, top, low, middle, top], axis=0).T

    turn(dp)
    for k in range(1, NT):
        source = lax.rem(z - k + NZ, NZ) * 2 + core

        @pl.when(tensor != k)
        def _():
            pltpu.make_async_remote_copy(
                src_ref=relay, dst_ref=gathered.at[source], send_sem=gather_send.at[k],
                recv_sem=gather_recv.at[k], device_id=in_plane(k), device_id_type=MESH,
            ).wait_recv()

        passing.append(
            send(gathered.at[source], gathered.at[source], pass_send.at[k], pass_recv.at[k], sibling)
        )
    for k in range(1, NT):
        turn(lax.rem(z - k + NZ, NZ) * 2 + core)
    for k, copy in enumerate(passing):
        copy.wait_recv()
        turn(lax.rem(z - k + NZ, NZ) * 2 + other)
    gram = gathered[0]
    for d in range(1, 2 * NZ):
        gram = gram + gathered[d]
    inverse = inverse_factor(pltpu.roll(gram, LANES - block, 1))
    last = sum_far(1, RANK, far_copies)
    last.wait_recv()
    right = dot_nn(inverse, jnp.concatenate([halves[1, 0, 0:RANK, :], halves[1, 1, 0:RANK, :]], axis=1))
    right_ref[...] = right
    weights = lax.dot_general(inverse, right, (((0,), (0,)), ((), ())), precision=HIGH, preferred_element_type=F32)
    top, middle, low = split_three(weights)
    stacked_ref[...] = jnp.concatenate([top, top, middle, top, middle, low], axis=0)
    early_done()
    hand_done()
    for copy in sent:
        copy.wait_send()


def residual(g_ref, e_ref, turned, stacked_ref, right_ref, out_hbm, right_hbm, out_ref, out_sem, right_sem):
    blocks = turned.shape[0]
    block = out_ref.shape[0] // blocks
    copies = [pltpu.make_async_copy(right_ref, right_hbm, right_sem)]
    copies[0].start()
    each = blocks // PIECES
    for piece in range(PIECES):
        for d in range(piece * each, (piece + 1) * each):
            rows = pl.ds(d * block, block)
            approx = jnp.dot(turned[d], stacked_ref[...], preferred_element_type=F32)
            total = g_ref[rows, :].astype(F32) + e_ref[rows, :].astype(F32)
            out_ref[rows, :] = (total - approx[:block]).astype(jnp.bfloat16)
        rows = pl.ds(piece * each * block, each * block)
        copies.append(pltpu.make_async_copy(out_ref.at[rows], out_hbm.at[0, rows], out_sem.at[piece]))
        copies[-1].start()
    for copy in copies:
        copy.wait()


def per_device(gradient, error_in, q_start):
    rows, columns = gradient.shape[1:]
    block = rows // (2 * NZ)
    hbm = pl.BlockSpec(memory_space=pltpu.HBM)
    vmem = pl.BlockSpec(memory_space=pltpu.VMEM)
    dma = pltpu.SemaphoreType.DMA
    half = RANK + 8
    kept = pl.pallas_call(
        compress,
        out_shape=[
            jax.ShapeDtypeStruct((rows, columns), jnp.bfloat16),
            jax.ShapeDtypeStruct((rows, columns), jnp.bfloat16),
            jax.ShapeDtypeStruct((2 * NZ, LANES, 6 * RANK), jnp.bfloat16),
            jax.ShapeDtypeStruct((6 * RANK, columns), jnp.bfloat16),
            jax.ShapeDtypeStruct((RANK, columns), F32),
        ],
        in_specs=[hbm, hbm, hbm],
        out_specs=[vmem] * 5,
        scratch_shapes=[
            pltpu.VMEM((RANK, columns), F32),
            pltpu.VMEM((NT, 2, RANK, LANES), F32),
            pltpu.VMEM((NT, 2, RANK, LANES), F32),
            pltpu.VMEM((2, RANK, LANES), F32),
            pltpu.VMEM((2 * NZ, RANK, LANES), F32),
            pltpu.VMEM((RANK, LANES), F32),
            pltpu.VMEM((NZ, block, columns), F32),
            pltpu.VMEM((NZ, block, columns), F32),
            pltpu.VMEM((NZ, block, columns), F32),
            pltpu.VMEM((2, 8, block, columns), F32),
            pltpu.VMEM((LANES, columns), jnp.bfloat16),
            pltpu.VMEM((LANES, columns), jnp.bfloat16),
            pltpu.VMEM((LANES, columns), jnp.bfloat16),
            pltpu.VMEM((RANK, LANES), F32),
            pltpu.VMEM((NT, RANK, LANES), F32),
            pltpu.VMEM((2, 2 * half, LANES), F32),
            pltpu.VMEM((2, half, LANES), F32),
            pltpu.VMEM((2, 4, half, LANES), F32),
            pltpu.VMEM((2, 4, half, LANES), F32),
            pltpu.VMEM((2, 2, half, LANES), F32),
            pltpu.VMEM((RANK, LANES), F32),
            pltpu.VMEM((2 * NZ, RANK, LANES), F32),
            dma((2, NZ)),
            dma((NZ,)), dma((NZ,)),
            dma((2, 8, CHUNKS)), dma((2, 8, CHUNKS)),
            dma((NT,)), dma((NT,)),
            dma((2,)), dma((2,)),
            dma((2, 4)), dma((2, 4)),
            dma((2, 4)), dma((2, 4)),
            dma((2,)), dma((2,)),
            dma((NT,)), dma((NT,)),
            dma((2,)), dma((2 * NZ,)),
            dma((NT,)), dma, dma,
            dma, dma,
            dma((NT,)), dma((NT,)),
            dma((NZ,)), dma((NZ,)),
            pltpu.SemaphoreType.REGULAR, pltpu.SemaphoreType.REGULAR, pltpu.SemaphoreType.REGULAR((4,)),
        ],
        compiler_params=pltpu.CompilerParams(
            collective_id=0, has_side_effects=True, vmem_limit_bytes=49 * 2**20 + 2**18
        ),
        name="compress",
    )(gradient, error_in, q_start)
    return pl.pallas_call(
        residual,
        out_shape=[
            jax.ShapeDtypeStruct(gradient.shape, gradient.dtype),
            jax.ShapeDtypeStruct((RANK, columns), F32),
        ],
        in_specs=[vmem] * 5,
        out_specs=[hbm, hbm],
        scratch_shapes=[pltpu.VMEM((rows, columns), jnp.bfloat16), dma((PIECES,)), dma],
        compiler_params=pltpu.CompilerParams(vmem_limit_bytes=16 * 2**20),
        name="residual",
    )(*kept)


def solution(mesh):
    placed = (P("dp", None, "tensor"), P("dp", None, "tensor"), P(None, "tensor"))
    return jax.shard_map(
        per_device,
        mesh=mesh,
        in_specs=placed,
        out_specs=(P("dp", None, "tensor"), P(None, "tensor")),
        check_vma=False,
    )
```
